32 devices in a mesh: ctx: 8 (over z, x), ch: 4 (over y, core).
Axes of the slice: x: 2, y: 2, z: 4, core: 2. Of those that a mesh axis runs over, the one named last changes fastest.
Arguments:
- tokens: bfloat16 [2048, 8192], P('ctx', 'ch'), may hold values from -6 to 6
- in_weight: bfloat16 [8192, 3, 8192], P('ctx', None, 'ch'), may hold values from -0.0625 to 0.0625
- short_filter: bfloat16 [3, 3, 8192], P(None, None, 'ch'), may hold values from -3 to 3
- decay_rate: float32 [8192, 16], P('ch'), may hold values from 2.4414063e-05 to 0.0333333333
- residue: float32 [8192, 16], P('ch'), may hold values from -0.12 to 0.12
- skip_gain: float32 [8192], P('ch'), may hold values from -4 to 4
Outputs:
- filtered: bfloat16 [2048, 8192], P('ctx', 'ch')
The draws below stay inside these ranges and needn't reach their ends.
All inputs are finite; a program needn't handle non-finite values.
Results may differ from the reference program's by a relative error of at most 0.007.
Values may be sent and summed in bfloat16 or wider, within the bound.
A program may use at most 128 MiB of HBM per device.

```python
import jax
import jax.numpy as jnp
from jax import lax

D = 8192
MODES = 16
SHORT_K = 3
TOKENS = 2048


def draw_decay_rate(key, part):
    fast_log = jnp.log(1.0 / 30.0)
    slow_log = jnp.log(0.05 / TOKENS)
    spread = jax.random.uniform(key, (D, MODES), jnp.float32, slow_log, fast_log)
    return jnp.clip(jnp.exp(spread), 0.05 / TOKENS, 1.0 / 30.0).astype(jnp.float32)


def block_levels(stream_key, shape, cuts, smallest, largest):
    def one(position, blocks):
        draws = jax.random.uniform(jax.random.fold_in(jax.random.fold_in(stream_key, 6), position), (blocks,), jnp.float32, smallest / len(cuts), largest / len(cuts))
        return jnp.repeat(jnp.exp(draws), shape[position] // blocks).reshape((-1,) + (1,) * (len(shape) - position - 1))

    level = one(*cuts[0])
    for cut in cuts[1:]:
        level = level * one(*cut)
    return level


def normal_values(rng, dims, width, reach, cuts=(), held_as=jnp.bfloat16):
    values = jax.random.normal(rng, dims, jnp.float32) * width
    if len(cuts) > 0:
        values = block_levels(rng, dims, cuts, -0.22, 0.18) * values
    return jnp.clip(values, min=-reach, max=reach).astype(held_as)


def setup_inputs(seed: int = 0) -> dict:
    keys = jax.random.split(jax.random.key(seed), 7)
    return {
        "tokens": normal_values(keys[0], (TOKENS, D), 1.0, 6.0, ((0, 8), (1, 4))),
        "in_weight": normal_values(keys[1], (D, 3, D), D ** -0.5, 0.0625, ((0, 8), (2, 4))),
        "short_filter": normal_values(keys[2], (SHORT_K, 3, D), 0.6, 3.0, ((2, 4),)),
        "decay_rate": draw_decay_rate(jax.random.fold_in(keys[6], 71), 0),
        "residue": normal_values(keys[4], (D, MODES), 0.02, 0.12, ((0, 4),), jnp.float32),
        "skip_gain": normal_values(keys[5], (D,), 1.0, 4.0, ((0, 4),), jnp.float32),
    }


def reference(tokens, in_weight, short_filter, decay_rate, residue, skip_gain):
    flat_weight = in_weight.reshape(D, 3 * D)
    projected = jnp.dot(tokens, flat_weight, preferred_element_type=jnp.float32).astype(jnp.bfloat16)
    projected = projected.reshape(TOKENS, 3, D)
    prefix = jnp.zeros((SHORT_K - 1, 3, D), jnp.float32)
    padded = jnp.concatenate([prefix, projected.astype(jnp.float32)], axis=0)
    filter_taps = short_filter.astype(jnp.float32)
    featured = jnp.zeros((TOKENS, 3, D), jnp.float32)
    for shift_back in range(SHORT_K):
        begin = SHORT_K - 1 - shift_back
        featured = featured + filter_taps[shift_back][None] * padded[begin:begin + TOKENS]
    query_gate = featured[:, 0]
    gated_rows = (featured[:, 1] * featured[:, 2]).astype(jnp.bfloat16)
    gated_wide = gated_rows.astype(jnp.float32)
    decay_factor = jnp.exp(-decay_rate)

    def advance(mode_state, gated_row):
        mode_state = decay_factor * mode_state + gated_row[:, None]
        return mode_state, jnp.sum(residue * mode_state, axis=1)

    unused, convolved = lax.scan(advance, jnp.zeros((D, MODES), jnp.float32), gated_wide)
    long_mix = convolved + skip_gain[None, :] * gated_wide
    return (query_gate * long_mix).astype(jnp.bfloat16)
```

```python
import jax
import jax.numpy as jnp
from jax import lax
from jax.experimental import pallas as pl
from jax.experimental.pallas import tpu as pltpu
from jax.sharding import PartitionSpec as P

LINE = 4
VMEM_LIMIT = 40 * 1024 * 1024
STEPS = 8


def state_kernel(gated_ref, keep_ref, state_ref):
    modes = keep_ref.shape[0]

    def body(i, state):
        for u in range(STEPS):
            row = gated_ref[i * STEPS + u]
            state = tuple(keep_ref[m] * state[m] + row for m in range(modes))
        return state

    zero = jnp.zeros(keep_ref.shape[1:], jnp.float32)
    state = lax.fori_loop(0, gated_ref.shape[0] // STEPS, body, (zero,) * modes)
    for m in range(modes):
        state_ref[m] = state[m]


def mix_kernel(gated_ref, query_ref, keep_ref, residue_ref, skip_ref, enter_ref, out_ref):
    modes = keep_ref.shape[0]

    def body(i, state):
        for u in range(STEPS):
            t = i * STEPS + u
            row = gated_ref[t]
            state = tuple(keep_ref[m] * state[m] + row for m in range(modes))
            terms = [residue_ref[m] * state[m] for m in range(modes)]
            terms.append(skip_ref[...] * row)
            while len(terms) > 1:
                terms = [sum(terms[k : k + 2][1:], terms[k]) for k in range(0, len(terms), 2)]
            out_ref[t] = query_ref[t] * terms[0]
        return state

    start = tuple(enter_ref[m] for m in range(modes))
    lax.fori_loop(0, gated_ref.shape[0] // STEPS, body, start)


def call(kernel, out_shape, count):
    return pl.pallas_call(
        kernel,
        out_shape=jax.ShapeDtypeStruct(out_shape, jnp.float32),
        in_specs=[pl.BlockSpec(memory_space=pltpu.VMEM)] * count,
        out_specs=pl.BlockSpec(memory_space=pltpu.VMEM),
        compiler_params=pltpu.CompilerParams(vmem_limit_bytes=VMEM_LIMIT),
    )


def local(tokens, in_weight, short_filter, decay_rate, residue, skip_gain):
    n_ctx, n_ch = lax.axis_size("ctx"), lax.axis_size("ch")
    n_x = n_ctx // LINE
    n_q = n_ch // LINE
    me = lax.axis_index("ctx")
    z, x = me // n_x, me % n_x
    tok_rows = tokens.shape[0]
    feats, streams, width = in_weight.shape
    part = width // n_x
    rows = tok_rows * n_x
    modes = decay_rate.shape[1]

    def along_z(block, hop):
        route = [
            (i * n_x + k, (i + hop) * n_x + k)
            for i in range(LINE)
            if 0 <= i + hop < LINE
            for k in range(n_x)
        ]
        return lax.ppermute(block, "ctx", route)

    def along_x(block, hop):
        route = [
            (i * n_x + k, i * n_x + (k + hop) % n_x) for i in range(LINE) for k in range(n_x)
        ]
        return lax.ppermute(block, "ctx", route)

    def weight_part(g, index):
        return lax.dynamic_slice_in_dim(in_weight[:, g], index * part, part, axis=1)

    weights = [[None] * n_x for g in range(streams)]
    for g in range(streams):
        for hop in range(1, n_x):
            weights[g][hop] = along_x(weight_part(g, (x + hop) % n_x), hop)
        weights[g][0] = weight_part(g, x)

    route = [
        ((i * n_x + k) * n_ch + a * n_q + q, (a * n_x + k) * n_ch + i * n_q + q)
        for i in range(LINE)
        for k in range(n_x)
        for a in range(LINE)
        for q in range(n_q)
    ]
    moved = lax.ppermute(tokens, ("ctx", "ch"), route)
    groups = [[i * n_x + k for k in range(n_x)] for i in range(LINE)]
    moved = lax.all_gather(moved, "ctx", axis_index_groups=groups)
    moved = lax.all_gather(moved, "ch")
    moved = moved.reshape(LINE, n_q, n_x, tok_rows, tokens.shape[1])
    plane = moved.transpose(0, 2, 3, 1, 4).reshape(LINE, rows, n_x * feats)

    def columns(hop):
        return lax.dynamic_slice_in_dim(plane, ((x - hop) % n_x) * feats, feats, axis=2)

    columns_by_hop = [columns(hop) for hop in range(n_x)]

    def share(g, index):
        total = None
        for hop in range(n_x):
            block = lax.dynamic_index_in_dim(columns_by_hop[hop], index, 0, keepdims=False)
            term = jnp.dot(block, weights[g][hop], preferred_element_type=jnp.float32)
            total = term if total is None else total + term
        return total

    def choose(values):
        return jnp.array(values, jnp.int32)[z]

    first = choose([3, 3, 0, 0])
    second = choose([2, 3, 0, 1])
    third_up = choose([1, 2, 3, 3])
    third_down = choose([0, 0, 1, 2])

    def reduce_stream(g):
        low = jnp.bfloat16
        send = share(g, first).astype(low)
        up, down = along_z(send, 1), along_z(send, -1)
        mine = share(g, second)
        up = along_z((mine + up.astype(jnp.float32)).astype(low), 1)
        down = along_z((mine + down.astype(jnp.float32)).astype(low), -1)
        up = along_z((share(g, third_up) + up.astype(jnp.float32)).astype(low), 1)
        down = along_z((share(g, third_down) + down.astype(jnp.float32)).astype(low), -1)
        return share(g, z) + up.astype(jnp.float32) + down.astype(jnp.float32)

    taps = lax.dynamic_slice_in_dim(short_filter, x * part, part, axis=2).astype(jnp.float32)
    tap_count = taps.shape[0]
    featured = []
    for g in range(streams):
        projected = reduce_stream(g)
        before = along_z(projected[rows - (tap_count - 1) :], 1)
        padded = jnp.concatenate([before, projected], axis=0)
        total = jnp.zeros(projected.shape, jnp.float32)
        for back in range(tap_count):
            begin = tap_count - 1 - back
            total = total + taps[back, g][None] * padded[begin : begin + rows]
        featured.append(total)

    lanes = 128
    tile = (part // lanes, lanes)
    query = featured[0].reshape((rows,) + tile)
    gated = (featured[1] * featured[2]).reshape((rows,) + tile)

    def by_mode(array):
        mine = lax.dynamic_slice_in_dim(array, x * part, part, axis=0)
        return mine.T.reshape((modes,) + tile)

    rate, weight = by_mode(decay_rate), by_mode(residue)
    skip = lax.dynamic_slice_in_dim(skip_gain, x * part, part, axis=0).reshape(tile)
    keep = jnp.exp(-rate)
    state = call(state_kernel, (modes,) + tile, 2)(gated, keep)
    enter = jnp.zeros_like(state)
    for hop in range(1, LINE):
        enter = enter + along_z(state, hop) * jnp.exp(-rate * float((hop - 1) * rows))
    mixed = call(mix_kernel, (rows,) + tile, 6)(gated, query, keep, weight, skip, enter)
    mixed = mixed.reshape(n_x, tok_rows, part).astype(jnp.bfloat16)

    out = jnp.zeros((tok_rows, width), jnp.bfloat16)
    for hop in range(n_x):
        block = lax.dynamic_index_in_dim(mixed, (x + hop) % n_x, 0, keepdims=False)
        if hop:
            block = along_x(block, hop)
        out = lax.dynamic_update_slice_in_dim(out, block, ((x - hop) % n_x) * part, axis=1)
    return out


def solution(mesh):
    in_specs = (
        P("ctx", "ch"),
        P("ctx", None, "ch"),
        P(None, None, "ch"),
        P("ch", None),
        P("ch", None),
        P("ch"),
    )
    out_specs = P("ctx", "ch")
    return jax.shard_map(local, mesh=mesh, in_specs=in_specs, out_specs=out_specs, check_vma=False)
```

```python
import jax
import jax.numpy as jnp
from jax import lax
from jax.experimental import pallas as pl
from jax.experimental.pallas import tpu as pltpu
from jax.sharding import PartitionSpec as P

LINE = 4
VMEM_LIMIT = 40 * 1024 * 1024
STEPS = 8


def state_kernel(gated_ref, keep_ref, state_ref):
    modes = keep_ref.shape[0]

    def body(i, state):
        for u in range(STEPS):
            row = gated_ref[i * STEPS + u]
            state = tuple(keep_ref[m] * state[m] + row for m in range(modes))
        return state

    zero = jnp.zeros(keep_ref.shape[1:], jnp.float32)
    state = lax.fori_loop(0, gated_ref.shape[0] // STEPS, body, (zero,) * modes)
    for m in range(modes):
        state_ref[m] = state[m]


def mix_kernel(gated_ref, query_ref, keep_ref, residue_ref, skip_ref, enter_ref, out_ref):
    modes = keep_ref.shape[0]

    def body(i, state):
        for u in range(STEPS):
            t = i * STEPS + u
            row = gated_ref[t]
            state = tuple(keep_ref[m] * state[m] + row for m in range(modes))
            terms = [residue_ref[m] * state[m] for m in range(modes)]
            terms.append(skip_ref[...] * row)
            while len(terms) > 1:
                terms = [sum(terms[k : k + 2][1:], terms[k]) for k in range(0, len(terms), 2)]
            out_ref[t] = query_ref[t] * terms[0]
        return state

    start = tuple(enter_ref[m] for m in range(modes))
    lax.fori_loop(0, gated_ref.shape[0] // STEPS, body, start)


def rolled(array, x, feats, n_x):
    result = array
    for k in range(1, n_x):
        result = jnp.where(x == k, jnp.roll(array, -k * feats, axis=-1), result)
    return result


def call(kernel, out_shape, count):
    return pl.pallas_call(
        kernel,
        out_shape=jax.ShapeDtypeStruct(out_shape, jnp.float32),
        in_specs=[pl.BlockSpec(memory_space=pltpu.VMEM)] * count,
        out_specs=pl.BlockSpec(memory_space=pltpu.VMEM),
        compiler_params=pltpu.CompilerParams(vmem_limit_bytes=VMEM_LIMIT),
    )


def local(tokens, in_weight, short_filter, decay_rate, residue, skip_gain):
    n_ctx, n_ch = lax.axis_size("ctx"), lax.axis_size("ch")
    n_x = n_ctx // LINE
    n_q = n_ch // LINE
    me = lax.axis_index("ctx")
    z, x = me // n_x, me % n_x
    tok_rows = tokens.shape[0]
    feats, streams, width = in_weight.shape
    part = width // n_x
    rows = tok_rows * n_x
    modes = decay_rate.shape[1]

    def along_z(block, hop):
        route = [
            (i * n_x + k, (i + hop) * n_x + k)
            for i in range(LINE)
            if 0 <= i + hop < LINE
            for k in range(n_x)
        ]
        return lax.ppermute(block, "ctx", route)

    def along_x(block, hop):
        route = [
            (i * n_x + k, i * n_x + (k + hop) % n_x) for i in range(LINE) for k in range(n_x)
        ]
        return lax.ppermute(block, "ctx", route)

    def weight_part(g, index):
        return lax.dynamic_slice_in_dim(in_weight[:, g], index * part, part, axis=1)

    away = [[weight_part(g, (x + hop) % n_x) for hop in range(1, n_x)] for g in range(streams)]

    def exchange(g):
        return [along_x(block, hop) for hop, block in enumerate(away[g], 1)]

    route = [
        ((i * n_x + k) * n_ch + a * n_q + q, (a * n_x + k) * n_ch + i * n_q + q)
        for i in range(LINE)
        for k in range(n_x)
        for a in range(LINE)
        for q in range(n_q)
    ]
    moved = lax.ppermute(tokens, ("ctx", "ch"), route)
    came = [exchange(0)]
    beside = jnp.zeros((n_x,) + moved.shape, moved.dtype)
    for hop in range(n_x):
        block = along_x(moved, hop) if hop else moved
        beside = lax.dynamic_update_index_in_dim(beside, block, (x - hop) % n_x, 0)
    if n_q == 1:
        beside = rolled(beside, x, feats, n_x)
    beside, away[1:] = lax.optimization_barrier((beside, away[1:]))
    came += [exchange(g) for g in range(1, streams)]
    gathered = lax.all_gather(beside, "ch")
    gathered = gathered.reshape(LINE, n_q, n_x, tok_rows, tokens.shape[1])
    plane = gathered.transpose(0, 2, 3, 1, 4).reshape(LINE, rows, n_x * feats)
    if n_q > 1:
        plane = rolled(plane, x, feats, n_x)

    weights = [
        jnp.concatenate([weight_part(g, x)] + came[g][::-1], axis=0) for g in range(streams)
    ]

    def share(g, index, source):
        block = lax.dynamic_index_in_dim(source, index, 0, keepdims=False)
        return jnp.dot(block, weights[g], preferred_element_type=jnp.float32)

    def choose(values):
        return sum(jnp.where(z == i, value, 0) for i, value in enumerate(values))

    def hops(block, pairs):
        return lax.ppermute(
            block, "ctx", [(i * n_x + k, j * n_x + k) for i, j in pairs for k in range(n_x)]
        )

    first = choose([3, 3, 0, 0])
    second = choose([2, 3, 0, 1])
    third_up = choose([1, 2, 3, 3])
    third_down = choose([0, 0, 1, 2])
    low, wide = jnp.bfloat16, jnp.float32

    def reduce_stream(g):
        one = hops(share(g, first, plane).astype(low), [(0, 1), (3, 2)])
        two = (share(g, second, plane) + one.astype(wide)).astype(low)
        two, later = lax.optimization_barrier((two, plane))
        up, down = hops(two, [(0, 1), (1, 2)]), hops(two, [(3, 2), (2, 1)])
        up = (share(g, third_up, later) + up.astype(wide)).astype(low)
        down = (share(g, third_down, later) + down.astype(wide)).astype(low)
        up, down, later = lax.optimization_barrier((up, down, later))
        up, down = hops(up, [(0, 1), (1, 2), (2, 3)]), hops(down, [(3, 2), (2, 1), (1, 0)])
        return share(g, z, later) + up.astype(wide) + down.astype(wide)

    taps = lax.dynamic_slice_in_dim(short_filter, x * part, part, axis=2).astype(jnp.float32)
    tap_count = taps.shape[0]
    featured = []
    for g in range(streams):
        projected = reduce_stream(g)
        before = along_z(projected[rows - (tap_count - 1) :], 1)
        padded = jnp.concatenate([before, projected], axis=0)
        total = jnp.zeros(projected.shape, jnp.float32)
        for back in range(tap_count):
            begin = tap_count - 1 - back
            total = total + taps[back, g][None] * padded[begin : begin + rows]
        featured.append(total)

    lanes = 128
    tile = (part // lanes, lanes)
    query = featured[0].reshape((rows,) + tile)
    gated = (featured[1] * featured[2]).reshape((rows,) + tile)

    def by_mode(array):
        mine = lax.dynamic_slice_in_dim(array, x * part, part, axis=0)
        return mine.T.reshape((modes,) + tile)

    rate, weight = by_mode(decay_rate), by_mode(residue)
    skip = lax.dynamic_slice_in_dim(skip_gain, x * part, part, axis=0).reshape(tile)
    keep = jnp.exp(-rate)
    state = call(state_kernel, (modes,) + tile, 2)(gated, keep)
    enter = jnp.zeros_like(state)
    for hop in range(1, LINE):
        enter = enter + along_z(state, hop) * jnp.exp(-rate * float((hop - 1) * rows))
    mixed = call(mix_kernel, (rows,) + tile, 6)(gated, query, keep, weight, skip, enter)
    mixed = mixed.reshape(n_x, tok_rows, part).astype(jnp.bfloat16)

    out = jnp.zeros((tok_rows, width), jnp.bfloat16)
    for hop in range(n_x):
        block = lax.dynamic_index_in_dim(mixed, (x + hop) % n_x, 0, keepdims=False)
        if hop:
            block = along_x(block, hop)
        out = lax.dynamic_update_slice_in_dim(out, block, ((x - hop) % n_x) * part, axis=1)
    return out


def solution(mesh):
    in_specs = (
        P("ctx", "ch"),
        P("ctx", None, "ch"),
        P(None, None, "ch"),
        P("ch", None),
        P("ch", None),
        P("ch"),
    )
    out_specs = P("ctx", "ch")
    return jax.shard_map(local, mesh=mesh, in_specs=in_specs, out_specs=out_specs, check_vma=False)
```

```python
import jax
import jax.numpy as jnp
from jax import lax
from jax.experimental import pallas as pl
from jax.experimental.pallas import tpu as pltpu
from jax.sharding import PartitionSpec as P

LINE = 4
CORES = 2
VMEM_LIMIT = 40 * 1024 * 1024
STEPS = 8


def state_kernel(gated_ref, keep_ref, state_ref):
    modes = keep_ref.shape[0]

    def body(i, state):
        for u in range(STEPS):
            row = gated_ref[i * STEPS + u]
            state = tuple(keep_ref[m] * state[m] + row for m in range(modes))
        return state

    zero = jnp.zeros(keep_ref.shape[1:], jnp.float32)
    state = lax.fori_loop(0, gated_ref.shape[0] // STEPS, body, (zero,) * modes)
    for m in range(modes):
        state_ref[m] = state[m]


def mix_kernel(gated_ref, query_ref, keep_ref, residue_ref, skip_ref, enter_ref, out_ref):
    modes = keep_ref.shape[0]

    def body(i, state):
        for u in range(STEPS):
            t = i * STEPS + u
            row = gated_ref[t]
            state = tuple(keep_ref[m] * state[m] + row for m in range(modes))
            terms = [residue_ref[m] * state[m] for m in range(modes)]
            terms.append(skip_ref[...] * row)
            while len(terms) > 1:
                terms = [sum(terms[k : k + 2][1:], terms[k]) for k in range(0, len(terms), 2)]
            out_ref[t] = query_ref[t] * terms[0]
        return state

    start = tuple(enter_ref[m] for m in range(modes))
    lax.fori_loop(0, gated_ref.shape[0] // STEPS, body, start)


def rolled(array, x, feats, n_x):
    result = array
    for k in range(1, n_x):
        result = jnp.where(x == k, jnp.roll(array, -k * feats, axis=-1), result)
    return result


def call(kernel, out_shape, count):
    return pl.pallas_call(
        kernel,
        out_shape=jax.ShapeDtypeStruct(out_shape, jnp.float32),
        in_specs=[pl.BlockSpec(memory_space=pltpu.VMEM)] * count,
        out_specs=pl.BlockSpec(memory_space=pltpu.VMEM),
        compiler_params=pltpu.CompilerParams(vmem_limit_bytes=VMEM_LIMIT),
    )


def local(tokens, in_weight, short_filter, decay_rate, residue, skip_gain):
    n_ctx, n_ch = lax.axis_size("ctx"), lax.axis_size("ch")
    n_x = n_ctx // LINE
    n_q = n_ch // LINE
    me = lax.axis_index("ctx")
    z, x = me // n_x, me % n_x
    tok_rows = tokens.shape[0]
    feats, streams, width = in_weight.shape
    part = width // n_x
    rows = tok_rows * n_x
    modes = decay_rate.shape[1]

    def along_z(block, hop):
        route = [
            (i * n_x + k, (i + hop) * n_x + k)
            for i in range(LINE)
            if 0 <= i + hop < LINE
            for k in range(n_x)
        ]
        return lax.ppermute(block, "ctx", route)

    def along_x(block, hop):
        route = [
            (i * n_x + k, i * n_x + (k + hop) % n_x) for i in range(LINE) for k in range(n_x)
        ]
        return lax.ppermute(block, "ctx", route)

    def weight_part(g, index):
        return lax.dynamic_slice_in_dim(in_weight[:, g], index * part, part, axis=1)

    away = [[weight_part(g, (x + hop) % n_x) for hop in range(1, n_x)] for g in range(streams)]

    def exchange(g):
        return [along_x(block, hop) for hop, block in enumerate(away[g], 1)]

    route = [
        ((i * n_x + k) * n_ch + a * n_q + q, (a * n_x + k) * n_ch + i * n_q + q)
        for i in range(LINE)
        for k in range(n_x)
        for a in range(LINE)
        for q in range(n_q)
    ]
    moved = lax.ppermute(tokens, ("ctx", "ch"), route)
    moved, away[0] = lax.optimization_barrier((moved, away[0]))
    came = [exchange(0)]
    beside = [along_x(moved, hop) if hop else moved for hop in range(n_x)]
    if n_q == 1:
        beside = [rolled(block, x, feats, n_x) for block in beside]

    mine = lax.axis_index("ch")
    outer = n_ch // CORES

    def along_outer(block, hop):
        route = [(i, (i + hop * CORES) % n_ch) for i in range(n_ch)]
        return lax.ppermute(block, "ch", route)

    def other_core(block):
        return lax.ppermute(block, "ch", [(i, i ^ 1) for i in range(n_ch)])

    found = jnp.zeros((n_ch, n_x) + moved.shape, moved.dtype)
    for hop in range(n_x):
        for step in range(outer):
            block = along_outer(beside[hop], step) if step else beside[hop]
            source = (mine - step * CORES) % n_ch
            for core, piece in enumerate((block, other_core(block))):
                owner = source + core * (1 - 2 * (mine % CORES))
                found = lax.dynamic_update_slice(
                    found, piece[None, None], (owner, (x - hop) % n_x, 0, 0)
                )
    beside, away[1:] = lax.optimization_barrier((beside, away[1:]))
    came += [exchange(g) for g in range(1, streams)]
    found = found.reshape(LINE, n_q, n_x, tok_rows, tokens.shape[1])
    plane = found.transpose(0, 2, 3, 1, 4).reshape(LINE, rows, n_x * feats)
    if n_q > 1:
        plane = rolled(plane, x, feats, n_x)

    weights = [
        jnp.concatenate([weight_part(g, x)] + came[g][::-1], axis=0) for g in range(streams)
    ]

    def share(g, index, source):
        block = lax.dynamic_index_in_dim(source, index, 0, keepdims=False)
        return jnp.dot(block, weights[g], preferred_element_type=jnp.float32)

    def choose(values):
        return sum(jnp.where(z == i, value, 0) for i, value in enumerate(values))

    def hops(block, pairs):
        return lax.ppermute(
            block, "ctx", [(i * n_x + k, j * n_x + k) for i, j in pairs for k in range(n_x)]
        )

    first = choose([3, 3, 0, 0])
    second = choose([2, 3, 0, 1])
    third_up = choose([1, 2, 3, 3])
    third_down = choose([0, 0, 1, 2])
    low, wide = jnp.bfloat16, jnp.float32

    def reduce_stream(g):
        one = hops(share(g, first, plane).astype(low), [(0, 1), (3, 2)])
        two = (share(g, second, plane) + one.astype(wide)).astype(low)
        two, later = lax.optimization_barrier((two, plane))
        up, down = hops(two, [(0, 1), (1, 2)]), hops(two, [(3, 2), (2, 1)])
        up = (share(g, third_up, later) + up.astype(wide)).astype(low)
        down = (share(g, third_down, later) + down.astype(wide)).astype(low)
        up, down, later = lax.optimization_barrier((up, down, later))
        up, down = hops(up, [(0, 1), (1, 2), (2, 3)]), hops(down, [(3, 2), (2, 1), (1, 0)])
        return share(g, z, later) + up.astype(wide) + down.astype(wide)

    taps = lax.dynamic_slice_in_dim(short_filter, x * part, part, axis=2).astype(jnp.float32)
    tap_count = taps.shape[0]
    projected = [reduce_stream(g) for g in range(streams)]
    halo = along_z(jnp.stack([sums[rows - (tap_count - 1) :] for sums in projected]), 1)
    featured = []
    for g in range(streams):
        padded = jnp.concatenate([halo[g], projected[g]], axis=0)
        total = jnp.zeros((rows, part), jnp.float32)
        for back in range(tap_count):
            begin = tap_count - 1 - back
            total = total + taps[back, g][None] * padded[begin : begin + rows]
        featured.append(total)

    lanes = 128
    tile = (part // lanes, lanes)
    query = featured[0].reshape((rows,) + tile)
    gated = (featured[1] * featured[2]).reshape((rows,) + tile)

    def by_mode(array):
        mine = lax.dynamic_slice_in_dim(array, x * part, part, axis=0)
        return mine.T.reshape((modes,) + tile)

    rate, weight = by_mode(decay_rate), by_mode(residue)
    skip = lax.dynamic_slice_in_dim(skip_gain, x * part, part, axis=0).reshape(tile)
    keep = jnp.exp(-rate)
    state = call(state_kernel, (modes,) + tile, 2)(gated, keep)
    enter = jnp.zeros_like(state)
    for hop in range(1, LINE):
        enter = enter + along_z(state, hop) * jnp.exp(-rate * float((hop - 1) * rows))
    mixed = call(mix_kernel, (rows,) + tile, 6)(gated, query, keep, weight, skip, enter)
    mixed = mixed.reshape(n_x, tok_rows, part).astype(jnp.bfloat16)

    out = jnp.zeros((tok_rows, width), jnp.bfloat16)
    for hop in range(n_x):
        block = lax.dynamic_index_in_dim(mixed, (x + hop) % n_x, 0, keepdims=False)
        if hop:
            block = along_x(block, hop)
        out = lax.dynamic_update_slice_in_dim(out, block, ((x - hop) % n_x) * part, axis=1)
    return out


def solution(mesh):
    in_specs = (
        P("ctx", "ch"),
        P("ctx", None, "ch"),
        P(None, None, "ch"),
        P("ch", None),
        P("ch", None),
        P("ch"),
    )
    out_specs = P("ctx", "ch")
    return jax.shard_map(local, mesh=mesh, in_specs=in_specs, out_specs=out_specs, check_vma=False)
```

```python
import jax
import jax.numpy as jnp
from jax import lax
from jax.experimental import pallas as pl
from jax.experimental.pallas import tpu as pltpu
from jax.sharding import PartitionSpec as P

LINE = 4
CORES = 2
VMEM_LIMIT = 40 * 1024 * 1024
STEPS = 8


def state_kernel(gated_ref, keep_ref, state_ref):
    modes = keep_ref.shape[0]

    def body(i, state):
        for u in range(STEPS):
            row = gated_ref[i * STEPS + u]
            state = tuple(keep_ref[m] * state[m] + row for m in range(modes))
        return state

    zero = jnp.zeros(keep_ref.shape[1:], jnp.float32)
    state = lax.fori_loop(0, gated_ref.shape[0] // STEPS, body, (zero,) * modes)
    for m in range(modes):
        state_ref[m] = state[m]


def mix_kernel(gated_ref, query_ref, keep_ref, residue_ref, skip_ref, enter_ref, out_ref):
    modes = keep_ref.shape[0]

    def body(i, state):
        for u in range(STEPS):
            t = i * STEPS + u
            row = gated_ref[t]
            state = tuple(keep_ref[m] * state[m] + row for m in range(modes))
            terms = [residue_ref[m] * state[m] for m in range(modes)]
            terms.append(skip_ref[...] * row)
            while len(terms) > 1:
                terms = [sum(terms[k : k + 2][1:], terms[k]) for k in range(0, len(terms), 2)]
            out_ref[t] = query_ref[t] * terms[0]
        return state

    start = tuple(enter_ref[m] for m in range(modes))
    lax.fori_loop(0, gated_ref.shape[0] // STEPS, body, start)


def rolled(array, x, feats, n_x):
    result = array
    for k in range(1, n_x):
        result = jnp.where(x == k, jnp.roll(array, -k * feats, axis=-1), result)
    return result


def call(kernel, out_shape, count):
    return pl.pallas_call(
        kernel,
        out_shape=jax.ShapeDtypeStruct(out_shape, jnp.float32),
        in_specs=[pl.BlockSpec(memory_space=pltpu.VMEM)] * count,
        out_specs=pl.BlockSpec(memory_space=pltpu.VMEM),
        compiler_params=pltpu.CompilerParams(vmem_limit_bytes=VMEM_LIMIT),
    )


def local(tokens, in_weight, short_filter, decay_rate, residue, skip_gain):
    n_ctx, n_ch = lax.axis_size("ctx"), lax.axis_size("ch")
    n_x = n_ctx // LINE
    n_q = n_ch // LINE
    me = lax.axis_index("ctx")
    z, x = me // n_x, me % n_x
    tok_rows = tokens.shape[0]
    feats, streams, width = in_weight.shape
    part = width // n_x
    rows = tok_rows * n_x
    modes = decay_rate.shape[1]

    def along_z(block, hop):
        route = [
            (i * n_x + k, (i + hop) * n_x + k)
            for i in range(LINE)
            if 0 <= i + hop < LINE
            for k in range(n_x)
        ]
        return lax.ppermute(block, "ctx", route)

    def along_x(block, hop):
        route = [
            (i * n_x + k, i * n_x + (k + hop) % n_x) for i in range(LINE) for k in range(n_x)
        ]
        return lax.ppermute(block, "ctx", route)

    def weight_part(g, index):
        return lax.dynamic_slice_in_dim(in_weight[:, g], index * part, part, axis=1)

    away = [[weight_part(g, (x + hop) % n_x) for hop in range(1, n_x)] for g in range(streams)]

    def exchange(g):
        return [along_x(block, hop) for hop, block in enumerate(away[g], 1)]

    route = [
        ((i * n_x + k) * n_ch + a * n_q + q, (a * n_x + k) * n_ch + i * n_q + q)
        for i in range(LINE)
        for k in range(n_x)
        for a in range(LINE)
        for q in range(n_q)
    ]
    moved = lax.ppermute(tokens, ("ctx", "ch"), route)
    moved, away[0] = lax.optimization_barrier((moved, away[0]))
    came = [exchange(0)]
    beside = [along_x(moved, hop) if hop else moved for hop in range(n_x)]
    if n_q == 1:
        beside = [rolled(block, x, feats, n_x) for block in beside]

    came[0], beside[1:], away[1] = lax.optimization_barrier((came[0], beside[1:], away[1]))
    came.append(exchange(1))

    mine = lax.axis_index("ch")
    outer = n_ch // CORES

    def along_outer(block, hop):
        route = [(i, (i + hop * CORES) % n_ch) for i in range(n_ch)]
        return lax.ppermute(block, "ch", route)

    def other_core(block):
        return lax.ppermute(block, "ch", [(i, i ^ 1) for i in range(n_ch)])

    found = jnp.zeros((n_ch, n_x) + moved.shape, moved.dtype)
    for hop in range(n_x):
        for step in range(outer):
            block = along_outer(beside[hop], step) if step else beside[hop]
            source = (mine - step * CORES) % n_ch
            for core, piece in enumerate((block, other_core(block))):
                owner = source + core * (1 - 2 * (mine % CORES))
                found = lax.dynamic_update_slice(
                    found, piece[None, None], (owner, (x - hop) % n_x, 0, 0)
                )
    found, came[1], away[2] = lax.optimization_barrier((found, came[1], away[2]))
    came.append(exchange(2))
    found = found.reshape(LINE, n_q, n_x, tok_rows, tokens.shape[1])
    plane = found.transpose(0, 2, 3, 1, 4).reshape(LINE, rows, n_x * feats)
    if n_q > 1:
        plane = rolled(plane, x, feats, n_x)

    def gathered_weight(g):
        return jnp.concatenate([weight_part(g, x)] + came[g][::-1], axis=0)

    def share(weight, index, source):
        block = lax.dynamic_index_in_dim(source, index, 0, keepdims=False)
        return jnp.dot(block, weight, preferred_element_type=jnp.float32)

    def choose(values):
        return sum(jnp.where(z == i, value, 0) for i, value in enumerate(values))

    def hops(block, pairs):
        return lax.ppermute(
            block, "ctx", [(i * n_x + k, j * n_x + k) for i, j in pairs for k in range(n_x)]
        )

    first = choose([3, 3, 0, 0])
    second = choose([2, 3, 0, 1])
    third_up = choose([1, 2, 3, 3])
    third_down = choose([0, 0, 1, 2])
    low, wide = jnp.bfloat16, jnp.float32

    def reduce_stream(g):
        weight = gathered_weight(g)
        one = hops(share(weight, first, plane).astype(low), [(0, 1), (3, 2)])
        two = (share(weight, second, plane) + one.astype(wide)).astype(low)
        if g == 0:
            two, came[2] = lax.optimization_barrier((two, came[2]))
        two, later = lax.optimization_barrier((two, plane))
        up, down = hops(two, [(0, 1), (1, 2)]), hops(two, [(3, 2), (2, 1)])
        up = (share(weight, third_up, later) + up.astype(wide)).astype(low)
        down = (share(weight, third_down, later) + down.astype(wide)).astype(low)
        up, down, later = lax.optimization_barrier((up, down, later))
        up, down = hops(up, [(0, 1), (1, 2), (2, 3)]), hops(down, [(3, 2), (2, 1), (1, 0)])
        return share(weight, z, later) + up.astype(wide) + down.astype(wide)

    taps = lax.dynamic_slice_in_dim(short_filter, x * part, part, axis=2).astype(jnp.float32)
    tap_count = taps.shape[0]
    projected = [reduce_stream(g) for g in range(streams)]
    halo = along_z(jnp.stack([sums[rows - (tap_count - 1) :] for sums in projected]), 1)
    featured = []
    for g in range(streams):
        padded = jnp.concatenate([halo[g], projected[g]], axis=0)
        total = jnp.zeros((rows, part), jnp.float32)
        for back in range(tap_count):
            begin = tap_count - 1 - back
            total = total + taps[back, g][None] * padded[begin : begin + rows]
        featured.append(total)

    lanes = 128
    tile = (part // lanes, lanes)
    query = featured[0].reshape((rows,) + tile)
    gated = (featured[1] * featured[2]).reshape((rows,) + tile)

    def by_mode(array):
        mine = lax.dynamic_slice_in_dim(array, x * part, part, axis=0)
        return mine.T.reshape((modes,) + tile)

    rate, weight = by_mode(decay_rate), by_mode(residue)
    skip = lax.dynamic_slice_in_dim(skip_gain, x * part, part, axis=0).reshape(tile)
    keep = jnp.exp(-rate)
    state = call(state_kernel, (modes,) + tile, 2)(gated, keep)
    enter = jnp.zeros_like(state)
    for hop in range(1, LINE):
        enter = enter + along_z(state, hop) * jnp.exp(-rate * float((hop - 1) * rows))
    mixed = call(mix_kernel, (rows,) + tile, 6)(gated, query, keep, weight, skip, enter)
    mixed = mixed.reshape(n_x, tok_rows, part).astype(jnp.bfloat16)

    out = jnp.zeros((tok_rows, width), jnp.bfloat16)
    for hop in range(n_x):
        block = lax.dynamic_index_in_dim(mixed, (x + hop) % n_x, 0, keepdims=False)
        if hop:
            block = along_x(block, hop)
        out = lax.dynamic_update_slice_in_dim(out, block, ((x - hop) % n_x) * part, axis=1)
    return out


def solution(mesh):
    in_specs = (
        P("ctx", "ch"),
        P("ctx", None, "ch"),
        P(None, None, "ch"),
        P("ch", None),
        P("ch", None),
        P("ch"),
    )
    out_specs = P("ctx", "ch")
    return jax.shard_map(local, mesh=mesh, in_specs=in_specs, out_specs=out_specs, check_vma=False)
```

```python
import jax
import jax.numpy as jnp
from jax import lax
from jax.experimental import pallas as pl
from jax.experimental.pallas import tpu as pltpu
from jax.sharding import PartitionSpec as P

LINE = 4
CORES = 2
VMEM_LIMIT = 40 * 1024 * 1024
STEPS = 8


def state_kernel(gated_ref, keep_ref, state_ref):
    modes = keep_ref.shape[0]

    def body(i, state):
        for u in range(STEPS):
            row = gated_ref[i * STEPS + u]
            state = tuple(keep_ref[m] * state[m] + row for m in range(modes))
        return state

    zero = jnp.zeros(keep_ref.shape[1:], jnp.float32)
    state = lax.fori_loop(0, gated_ref.shape[0] // STEPS, body, (zero,) * modes)
    for m in range(modes):
        state_ref[m] = state[m]


def mix_kernel(gated_ref, query_ref, keep_ref, residue_ref, skip_ref, enter_ref, out_ref):
    modes = keep_ref.shape[0]

    def body(i, state):
        for u in range(STEPS):
            t = i * STEPS + u
            row = gated_ref[t]
            state = tuple(keep_ref[m] * state[m] + row for m in range(modes))
            terms = [residue_ref[m] * state[m] for m in range(modes)]
            terms.append(skip_ref[...] * row)
            while len(terms) > 1:
                terms = [sum(terms[k : k + 2][1:], terms[k]) for k in range(0, len(terms), 2)]
            out_ref[t] = query_ref[t] * terms[0]
        return state

    start = tuple(enter_ref[m] for m in range(modes))
    lax.fori_loop(0, gated_ref.shape[0] // STEPS, body, start)


def swapped(i):
    return (i % 2) * 2 + i // 2


def rolled(array, x, feats, n_x):
    result = array
    for k in range(1, n_x):
        result = jnp.where(x == k, jnp.roll(array, -k * feats, axis=-1), result)
    return result


def call(kernel, out_shape, count):
    return pl.pallas_call(
        kernel,
        out_shape=jax.ShapeDtypeStruct(out_shape, jnp.float32),
        in_specs=[pl.BlockSpec(memory_space=pltpu.VMEM)] * count,
        out_specs=pl.BlockSpec(memory_space=pltpu.VMEM),
        compiler_params=pltpu.CompilerParams(vmem_limit_bytes=VMEM_LIMIT),
    )


def local(tokens, in_weight, short_filter, decay_rate, residue, skip_gain):
    n_ctx, n_ch = lax.axis_size("ctx"), lax.axis_size("ch")
    n_x = n_ctx // LINE
    n_q = n_ch // LINE
    me = lax.axis_index("ctx")
    z, x = me // n_x, me % n_x
    tok_rows = tokens.shape[0]
    feats, streams, width = in_weight.shape
    part = width // n_x
    rows = tok_rows * n_x
    modes = decay_rate.shape[1]

    def along_z(block, hop):
        route = [
            (i * n_x + k, (i + hop) * n_x + k)
            for i in range(LINE)
            if 0 <= i + hop < LINE
            for k in range(n_x)
        ]
        return lax.ppermute(block, "ctx", route)

    def along_x(block, hop):
        route = [
            (i * n_x + k, i * n_x + (k + hop) % n_x) for i in range(LINE) for k in range(n_x)
        ]
        return lax.ppermute(block, "ctx", route)

    def weight_part(g, index):
        return lax.dynamic_slice_in_dim(in_weight[:, g], index * part, part, axis=1)

    away = [[weight_part(g, (x + hop) % n_x) for hop in range(1, n_x)] for g in range(streams)]

    def exchange(g):
        return [along_x(block, hop) for hop, block in enumerate(away[g], 1)]

    route = [
        ((i * n_x + k) * n_ch + a * n_q + q, (a * n_x + k) * n_ch + swapped(i) * n_q + q)
        for i in range(LINE)
        for k in range(n_x)
        for a in range(LINE)
        for q in range(n_q)
    ]
    moved = lax.ppermute(tokens, ("ctx", "ch"), route)
    moved, away[0] = lax.optimization_barrier((moved, away[0]))
    came = [exchange(0)]
    beside = [along_x(moved, hop) if hop else moved for hop in range(n_x)]
    if n_q == 1:
        beside = [rolled(block, x, feats, n_x) for block in beside]

    came[0], beside[1:], away[1] = lax.optimization_barrier((came[0], beside[1:], away[1]))
    came.append(exchange(1))

    mine = lax.axis_index("ch")
    outer = n_ch // CORES

    def along_outer(block, hop):
        route = [(i, (i + hop * CORES) % n_ch) for i in range(n_ch)]
        return lax.ppermute(block, "ch", route)

    def other_core(block):
        return lax.ppermute(block, "ch", [(i, i ^ 1) for i in range(n_ch)])

    found = jnp.zeros((n_ch, n_x) + moved.shape, moved.dtype)
    for hop in range(n_x):
        for step in range(outer):
            block = along_outer(beside[hop], step) if step else beside[hop]
            source = (mine - step * CORES) % n_ch
            for core, piece in enumerate((block, other_core(block))):
                owner = source + core * (1 - 2 * (mine % CORES))
                slot = swapped(owner // n_q) * n_q + owner % n_q
                found = lax.dynamic_update_slice(
                    found, piece[None, None], (slot, (x - hop) % n_x, 0, 0)
                )
    found, came[1], away[2] = lax.optimization_barrier((found, came[1], away[2]))
    came.append(exchange(2))
    found = found.reshape(LINE, n_q, n_x, tok_rows, tokens.shape[1])
    plane = found.transpose(0, 2, 3, 1, 4).reshape(LINE, rows, n_x * feats)
    if n_q > 1:
        plane = rolled(plane, x, feats, n_x)

    def gathered_weight(g):
        return jnp.concatenate([weight_part(g, x)] + came[g][::-1], axis=0)

    def share(weight, index, source):
        block = lax.dynamic_index_in_dim(source, index, 0, keepdims=False)
        return jnp.dot(block, weight, preferred_element_type=jnp.float32)

    def choose(values):
        return sum(jnp.where(z == i, value, 0) for i, value in enumerate(values))

    def hops(block, pairs):
        return lax.ppermute(
            block, "ctx", [(i * n_x + k, j * n_x + k) for i, j in pairs for k in range(n_x)]
        )

    first = choose([3, 3, 0, 0])
    second = choose([2, 3, 0, 1])
    third_up = choose([1, 2, 3, 3])
    third_down = choose([0, 0, 1, 2])
    low, wide = jnp.bfloat16, jnp.float32

    def reduce_stream(g):
        weight = gathered_weight(g)
        one = hops(share(weight, first, plane).astype(low), [(0, 1), (3, 2)])
        two = (share(weight, second, plane) + one.astype(wide)).astype(low)
        if g == 0:
            two, came[2] = lax.optimization_barrier((two, came[2]))
        two, later = lax.optimization_barrier((two, plane))
        up, down = hops(two, [(0, 1), (1, 2)]), hops(two, [(3, 2), (2, 1)])
        up = (share(weight, third_up, later) + up.astype(wide)).astype(low)
        down = (share(weight, third_down, later) + down.astype(wide)).astype(low)
        up, down, later = lax.optimization_barrier((up, down, later))
        up, down = hops(up, [(0, 1), (1, 2), (2, 3)]), hops(down, [(3, 2), (2, 1), (1, 0)])
        return share(weight, z, later) + up.astype(wide) + down.astype(wide)

    taps = lax.dynamic_slice_in_dim(short_filter, x * part, part, axis=2).astype(jnp.float32)
    tap_count = taps.shape[0]
    projected = [reduce_stream(g) for g in range(streams)]
    halo = along_z(jnp.stack([sums[rows - (tap_count - 1) :] for sums in projected]), 1)
    featured = []
    for g in range(streams):
        padded = jnp.concatenate([halo[g], projected[g]], axis=0)
        total = jnp.zeros((rows, part), jnp.float32)
        for back in range(tap_count):
            begin = tap_count - 1 - back
            total = total + taps[back, g][None] * padded[begin : begin + rows]
        featured.append(total)

    lanes = 128
    tile = (part // lanes, lanes)
    query = featured[0].reshape((rows,) + tile)
    gated = (featured[1] * featured[2]).reshape((rows,) + tile)

    def by_mode(array):
        mine = lax.dynamic_slice_in_dim(array, x * part, part, axis=0)
        return mine.T.reshape((modes,) + tile)

    rate, weight = by_mode(decay_rate), by_mode(residue)
    skip = lax.dynamic_slice_in_dim(skip_gain, x * part, part, axis=0).reshape(tile)
    keep = jnp.exp(-rate)
    state = call(state_kernel, (modes,) + tile, 2)(gated, keep)
    enter = jnp.zeros_like(state)
    for hop in range(1, LINE):
        enter = enter + along_z(state, hop) * jnp.exp(-rate * float((hop - 1) * rows))
    mixed = call(mix_kernel, (rows,) + tile, 6)(gated, query, keep, weight, skip, enter)
    mixed = mixed.reshape(n_x, tok_rows, part).astype(jnp.bfloat16)

    out = jnp.zeros((tok_rows, width), jnp.bfloat16)
    for hop in range(n_x):
        block = lax.dynamic_index_in_dim(mixed, (x + hop) % n_x, 0, keepdims=False)
        if hop:
            block = along_x(block, hop)
        out = lax.dynamic_update_slice_in_dim(out, block, ((x - hop) % n_x) * part, axis=1)
    return out


def solution(mesh):
    in_specs = (
        P("ctx", "ch"),
        P("ctx", None, "ch"),
        P(None, None, "ch"),
        P("ch", None),
        P("ch", None),
        P("ch"),
    )
    out_specs = P("ctx", "ch")
    return jax.shard_map(local, mesh=mesh, in_specs=in_specs, out_specs=out_specs, check_vma=False)
```
